256 devices in a mesh: sub: 64 (over z, y, core), blk: 4 (over x).
Axes of the slice: x: 4, y: 4, z: 8, core: 2. Of those that a mesh axis runs over, the one named last changes fastest.
Arguments:
- inputs: bfloat16 [16, 1048576], P(None, ('sub', 'blk')), may hold values from -6 to 6
- adjoint_in: bfloat16 [16, 1048576], P(None, ('sub', 'blk')), may hold values from -6 to 6
- panel_map: int32 [256, 4096], P(('sub', 'blk')), may hold values from 0 to 4095, each once within a row
- bases: bfloat16 [4096, 128, 256], P(('sub', 'blk')), may hold values from -0.375 to 0.375
- near_blocks: bfloat16 [4096, 256, 256], P(('sub', 'blk')), may hold values from -0.375 to 0.375
- transfers: bfloat16 [4096, 128, 128], P(('sub', 'blk')), may hold values from -0.125 to 0.125
- up_maps: bfloat16 [1536, 128, 128], P(('sub', 'blk')), may hold values from -0.5 to 0.5
- down_maps: bfloat16 [1536, 128, 128], P(('sub', 'blk')), may hold values from -0.5 to 0.5
- send_list: int32 [256, 128], P(('sub', 'blk')), may hold values from 0 to 15
- target_leaf: int32 [256, 128], P(('sub', 'blk')), may hold values from 0 to 15
- couplings: bfloat16 [32768, 128, 128], P(('sub', 'blk')), may hold values from -0.5 to 0.5
Outputs:
- product: bfloat16 [16, 1048576], P(None, ('sub', 'blk'))
- adjoint_product: bfloat16 [16, 1048576], P(None, ('sub', 'blk'))
The draws below stay inside these ranges and needn't reach their ends.
Inputs may be any that keep to these rules, and one draw needn't show every extreme that they name: `panel_map`: each row is a permutation of 0 to 4095. `send_list`: entries name leaves of the sending group. `target_leaf`: entries name leaves of the receiving group.
All inputs are finite; a program needn't handle non-finite values.
Results may differ from the reference program's by a relative error of at most 0.0059.
Values may be sent and summed in bfloat16 or wider, within the bound.
A program may use at most 64 MiB of HBM per device.

```python
import jax
import jax.numpy as jnp
from jax import lax

K = 128
P_SIZE = 256
RHS = 16
LEAF_DEV = 16
SLOTS = 2
LV = 6
PAN_DEV = 4096
PANELS = 1048576
N_SUB = 64
N_BLK = 4
DEVICES = 256


def touch_ends(array, rng, smallest, top_value):
    longest = array.shape.index(max(array.shape))
    spots = []
    for shift in (0, 1):
        where = [jax.random.randint(jax.random.fold_in(rng, axis), (), 0, length) for axis, length in enumerate(array.shape)]
        where[longest] = (where[longest] + shift) % array.shape[longest]
        spots.append(tuple(where))
    return array.at[spots[0]].set(smallest).at[spots[1]].set(top_value)


def steps_of(own_key, dims, cuts, smallest, top_value):
    loudness, own = 1.0, jax.random.fold_in(own_key, 6)
    for position, parts in cuts:
        draws = jnp.exp(jax.random.uniform(jax.random.fold_in(own, position), (parts,), jnp.float32, smallest / len(cuts), top_value / len(cuts)))
        loudness = loudness * jnp.repeat(draws, dims[position] // parts).reshape([-1 if axis == position else 1 for axis in range(len(dims))])
    return loudness


def gaussian(key, extent, width, limit, cuts=(), kind=jnp.bfloat16):
    array = width * jax.random.normal(key, extent, jnp.float32)
    if cuts:
        array = array * steps_of(key, extent, cuts, -0.22, 0.18)
    return jnp.clip(array, -limit, limit).astype(kind)


def setup_inputs(seed: int = 0) -> dict:
    key_list = jax.random.split(jax.random.key(seed), 12)
    inputs = gaussian(key_list[0], (RHS, PANELS), 1.0, 6.0, ((1, 256),))
    adjoint_in = gaussian(key_list[1], (RHS, PANELS), 1.0, 6.0, ((1, 256),))
    panel_map = jax.vmap(lambda own: jax.random.permutation(own, PAN_DEV))(jax.random.split(key_list[2], DEVICES)).reshape((DEVICES, PAN_DEV)).astype(jnp.int32)
    bases = gaussian(key_list[3], (DEVICES * LEAF_DEV, K, P_SIZE), P_SIZE ** -0.5, 0.375, ((0, 256),))
    near_blocks = gaussian(key_list[4], (DEVICES * LEAF_DEV, P_SIZE, P_SIZE), P_SIZE ** -0.5, 0.375, ((0, 256),))
    transfers = gaussian(key_list[5], (DEVICES * LEAF_DEV, K, K), (LEAF_DEV * K) ** -0.5, 0.125, ((0, 256),))
    up_maps = gaussian(key_list[6], (DEVICES * LV, K, K), K ** -0.5, 0.5, ((0, 256),))
    down_maps = gaussian(key_list[7], (DEVICES * LV, K, K), K ** -0.5, 0.5, ((0, 256),))
    send_list = touch_ends(jax.random.randint(key_list[8], (DEVICES, N_SUB * SLOTS), 0, LEAF_DEV), jax.random.fold_in(key_list[8], 1), 0, LEAF_DEV - 1).astype(jnp.int32)
    target_leaf = touch_ends(jax.random.randint(key_list[9], (DEVICES, N_SUB * SLOTS), 0, LEAF_DEV), jax.random.fold_in(key_list[9], 1), 0, LEAF_DEV - 1).astype(jnp.int32)
    couplings = gaussian(key_list[10], (DEVICES * N_SUB * SLOTS, K, K), K ** -0.5, 0.5, ((0, 256),))
    return dict(inputs=inputs, adjoint_in=adjoint_in, panel_map=panel_map, bases=bases, near_blocks=near_blocks, transfers=transfers, up_maps=up_maps, down_maps=down_maps, send_list=send_list, target_leaf=target_leaf, couplings=couplings)


HIGHEST = lax.Precision.HIGHEST


def sibling_weights():
    level_ids = jnp.arange(LV, dtype=jnp.int32)[:, None, None]
    row_ids = jnp.arange(N_SUB, dtype=jnp.int32)[None, :, None]
    col_ids = jnp.arange(N_SUB, dtype=jnp.int32)[None, None, :]
    match = jnp.right_shift(col_ids, level_ids) == jnp.bitwise_xor(jnp.right_shift(row_ids, level_ids), 1)
    return match.astype(jnp.float32)


def reroute(buffers):
    shape = buffers.shape
    split = buffers.reshape((N_SUB, N_BLK, N_SUB, SLOTS) + shape[2:])
    return jnp.swapaxes(split, 0, 2).reshape(shape)


def leaf_terms(pieces):
    forward, backward, ordering, basis_rows, near_part, transfer = pieces
    basis32 = basis_rows.astype(jnp.float32)
    near32 = near_part.astype(jnp.float32)
    transfer32 = transfer.astype(jnp.float32)
    fwd_panels = forward[:, ordering].reshape(RHS, LEAF_DEV, P_SIZE).astype(jnp.float32)
    bwd_panels = backward[:, ordering].reshape(RHS, LEAF_DEV, P_SIZE).astype(jnp.float32)
    fwd_skel = jnp.einsum('mlp,lkp->lmk', fwd_panels, basis32, precision=HIGHEST).astype(jnp.bfloat16)
    bwd_skel = jnp.einsum('mlp,lkp->lmk', bwd_panels, basis32, precision=HIGHEST).astype(jnp.bfloat16)
    near_fwd = jnp.einsum('mlq,lpq->mlp', fwd_panels, near32, precision=HIGHEST)
    near_bwd = jnp.einsum('mlp,lpq->mlq', bwd_panels, near32, precision=HIGHEST)
    fwd_group = jnp.einsum('lmk,ljk->mj', fwd_skel.astype(jnp.float32), transfer32, precision=HIGHEST)
    bwd_group = jnp.einsum('lmk,lkj->mj', bwd_skel.astype(jnp.float32), transfer32, precision=HIGHEST)
    return fwd_skel, bwd_skel, near_fwd, near_bwd, fwd_group, bwd_group


def list_terms(pieces):
    incoming, bwd_skel, targets, coupling = pieces
    coupling32 = coupling.astype(jnp.float32)
    terms = jnp.einsum('qmk,qik->qmi', incoming.astype(jnp.float32), coupling32, precision=HIGHEST)
    picked = jnp.take(bwd_skel, targets.astype(jnp.int32), axis=0).astype(jnp.float32)
    returned = jnp.einsum('qmi,qik->qmk', picked, coupling32, precision=HIGHEST).astype(jnp.bfloat16)
    onehot = (targets[:, None] == jnp.arange(LEAF_DEV, dtype=jnp.int32)[None, :]).astype(jnp.float32)
    summed = jnp.einsum('ql,qmi->lmi', onehot, terms, precision=HIGHEST)
    return summed, returned


def leaf_out(pieces):
    fwd_local, bwd_local, list_fwd, list_bwd, transfer, basis_rows, near_fwd, near_bwd, ordering = pieces
    transfer32 = transfer.astype(jnp.float32)
    basis32 = basis_rows.astype(jnp.float32)
    fwd_leaf = (jnp.einsum('mj,ljk->lmk', fwd_local, transfer32, precision=HIGHEST) + list_fwd).astype(jnp.bfloat16)
    bwd_leaf = (jnp.einsum('mj,lkj->lmk', bwd_local, transfer32, precision=HIGHEST) + list_bwd).astype(jnp.bfloat16)
    fwd_vals = jnp.einsum('lmk,lkp->mlp', fwd_leaf.astype(jnp.float32), basis32, precision=HIGHEST) + near_fwd
    bwd_vals = jnp.einsum('lmk,lkp->mlp', bwd_leaf.astype(jnp.float32), basis32, precision=HIGHEST) + near_bwd
    fwd_vals = fwd_vals.reshape(RHS, PAN_DEV).astype(jnp.bfloat16)
    bwd_vals = bwd_vals.reshape(RHS, PAN_DEV).astype(jnp.bfloat16)
    fwd_res = jnp.zeros((RHS, PAN_DEV), jnp.bfloat16).at[:, ordering].set(fwd_vals)
    bwd_res = jnp.zeros((RHS, PAN_DEV), jnp.bfloat16).at[:, ordering].set(bwd_vals)
    return fwd_res, bwd_res


def reference(inputs, adjoint_in, panel_map, bases, near_blocks, transfers, up_maps, down_maps, send_list, target_leaf, couplings):
    groups = N_SUB * N_BLK
    slot_count = N_SUB * SLOTS
    forward_dev = jnp.swapaxes(inputs.reshape(RHS, groups, PAN_DEV), 0, 1)
    backward_dev = jnp.swapaxes(adjoint_in.reshape(RHS, groups, PAN_DEV), 0, 1)
    basis_dev = bases.reshape(groups, LEAF_DEV, K, P_SIZE)
    near_dev = near_blocks.reshape(groups, LEAF_DEV, P_SIZE, P_SIZE)
    transfer_dev = transfers.reshape(groups, LEAF_DEV, K, K)
    up_dev = up_maps.reshape(groups, LV, K, K).astype(jnp.float32)
    down_dev = down_maps.reshape(groups, LV, K, K).astype(jnp.float32)
    coupling_dev = couplings.reshape(groups, slot_count, K, K)
    ordering = panel_map.astype(jnp.int32)
    fwd_skel, bwd_skel, near_fwd, near_bwd, fwd_group, bwd_group = lax.map(
        leaf_terms, (forward_dev, backward_dev, ordering, basis_dev, near_dev, transfer_dev))
    fwd_terms = jnp.einsum('dmj,dlij->dlmi', fwd_group, up_dev, precision=HIGHEST)
    bwd_terms = jnp.einsum('dmj,dlji->dlmi', bwd_group, down_dev, precision=HIGHEST)
    fwd_sub = fwd_terms.reshape(N_SUB, N_BLK, LV, RHS, K).sum(axis=1)
    bwd_sub = bwd_terms.reshape(N_SUB, N_BLK, LV, RHS, K).sum(axis=1)
    weights = sibling_weights()
    sib_fwd = jnp.repeat(jnp.einsum('lrs,slmk->rlmk', weights, fwd_sub, precision=HIGHEST), N_BLK, axis=0)
    sib_bwd = jnp.repeat(jnp.einsum('lrs,slmk->rlmk', weights, bwd_sub, precision=HIGHEST), N_BLK, axis=0)
    fwd_local = jnp.einsum('dlmi,dlji->dmj', sib_fwd, down_dev, precision=HIGHEST)
    bwd_local = jnp.einsum('dlmi,dlij->dmj', sib_bwd, up_dev, precision=HIGHEST)
    sources = send_list.astype(jnp.int32)
    outgoing = jnp.take_along_axis(fwd_skel, sources[:, :, None, None], axis=1)
    incoming = reroute(outgoing)
    list_fwd, returned_src = lax.map(list_terms, (incoming, bwd_skel, target_leaf.astype(jnp.int32), coupling_dev))
    returned = reroute(returned_src)
    onehot_src = (sources[:, :, None] == jnp.arange(LEAF_DEV, dtype=jnp.int32)[None, None, :]).astype(jnp.float32)
    list_bwd = jnp.einsum('dql,dqmk->dlmk', onehot_src, returned.astype(jnp.float32), precision=HIGHEST)
    product_dev, adjoint_dev = lax.map(leaf_out, (fwd_local, bwd_local, list_fwd, list_bwd, transfer_dev, basis_dev, near_fwd, near_bwd, ordering))
    product = jnp.swapaxes(product_dev, 0, 1).reshape(RHS, groups * PAN_DEV)
    adjoint_product = jnp.swapaxes(adjoint_dev, 0, 1).reshape(RHS, groups * PAN_DEV)
    return product, adjoint_product
```

```python
import jax
import jax.numpy as jnp
from jax import lax
from jax.experimental import pallas as pl
from jax.experimental.pallas import tpu as pltpu
from jax.sharding import PartitionSpec as P

F32 = jnp.float32
BF16 = jnp.bfloat16
MESH = pl.DeviceIdType.MESH

FWD = (0, 1, -1, 2, -2, 3, -3, 4)
BWD = (4, 3, -3, 2, -2, 1, -1, 0)
FPOS = {d: i for i, d in enumerate(FWD)}
BPOS = {d: i for i, d in enumerate(BWD)}
FBATCH = ((0, 3), (3, 5), (5, 7), (7, 8))
BBATCH = ((0, 1), (1, 3), (3, 5), (5, 8))


def nt(a, b):
    return lax.dot_general(a, b, (((1,), (1,)), ((), ())), preferred_element_type=F32)


def nn(a, b):
    return lax.dot_general(a, b, (((1,), (0,)), ((), ())), preferred_element_type=F32)


def batch_nt(a, b):
    return lax.dot_general(a, b, (((2,), (2,)), ((0,), (0,))), preferred_element_type=F32)


def batch_nn(a, b):
    return lax.dot_general(a, b, (((2,), (1,)), ((0,), (0,))), preferred_element_type=F32)


def split(a):
    high = a.astype(BF16)
    low = (a - high.astype(F32)).astype(BF16)
    return high, low


def stacked(a):
    high, low = split(a)
    return jnp.concatenate([high, low], axis=0)


def folded(a):
    half = a.shape[0] // 2
    return a[:half] + a[half:]


def xor3(a, e):
    total = 0
    for bit in range(3):
        value = lax.rem(a // (1 << bit), 2)
        if (e >> bit) & 1:
            value = 1 - value
        total = total + value * (1 << bit)
    return total


def level_of(e):
    return 0 if e == 1 else (1 if e < 4 else 2)


def kernel(
    inp, adj, pmap, slist, tlist,
    bases_h, near_h, trans_h, up_h, down_h, coup_h,
    out_x, out_a,
    bases, near, trans, up, down, coup,
    xl, oh, gath, nterm, diff_n, diff_t, acc,
    ag, ws, lists, fsend, frecv, bsend, brecv,
    cws, cwr, ccs, ccr,
    lxs, lxr, lws, lwr, lzs, lzr, lar,
    local_sem, ag_s, ag_r, list_s, list_r, f_s, f_r, b_s, b_r,
    cw_s, cw_r, cc_s, cc_r, lx_s, lx_r, lw_s, lw_r, lz_s, lz_r, la_s, la_r,
):
    s = lax.axis_index("sub")
    b = lax.axis_index("blk")
    z = s // 8
    w = lax.rem(s, 8)

    loads = []
    for i, (src, dst) in enumerate(
        ((bases_h, bases), (trans_h, trans), (up_h, up), (down_h, down), (coup_h, coup), (near_h, near))
    ):
        copy = pltpu.make_async_copy(src, dst, local_sem.at[i])
        copy.start()
        loads.append(copy)

    def z_dev(d):
        return (lax.rem(z + d + 8, 8) * 8 + w, b)

    def zx_dev(e):
        return (xor3(z, e) * 8 + w, b)

    def w_dev(e):
        return (z * 8 + xor3(w, e), b)

    def x_dev(d):
        return (s, lax.rem(b + d, 4))

    barrier = pltpu.get_barrier_semaphore()
    for e in range(1, 8):
        pl.semaphore_signal(barrier, inc=1, device_id=zx_dev(e), device_id_type=MESH)
        pl.semaphore_signal(barrier, inc=1, device_id=w_dev(e), device_id_type=MESH)
    for d in range(1, 4):
        pl.semaphore_signal(barrier, inc=1, device_id=x_dev(d), device_id_type=MESH)

    def send(src, dst, ssem, rsem, dev):
        copy = pltpu.make_async_remote_copy(
            src_ref=src, dst_ref=dst, send_sem=ssem, recv_sem=rsem, device_id=dev, device_id_type=MESH
        )
        copy.start()
        return copy

    sent = []

    row = lax.broadcasted_iota(jnp.int32, (256, 256), 0)
    col = lax.broadcasted_iota(jnp.int32, (256, 256), 1)
    diff_n[...] = (row - (col & 15)).astype(F32)
    diff_t[...] = (col - (row & 15)).astype(F32)
    for h in range(16):
        xl[h * 32 : h * 32 + 16, :] = inp[:, h * 256 : (h + 1) * 256]
        xl[h * 32 + 16 : h * 32 + 32, :] = adj[:, h * 256 : (h + 1) * 256]
    lists[0] = jnp.broadcast_to(slist[...].astype(F32), (16, 128)).astype(BF16)
    targets = jnp.broadcast_to(tlist[...].astype(F32), (16, 128))

    loads[0].wait()
    loads[1].wait()

    def leaf_in(leaf, carry):
        xd, wd = carry
        off = pl.multiple_of(leaf * 256, 256)
        places = pmap[:, pl.ds(off, 256)]
        low, high = places & 255, places >> 8
        hot = jnp.where(lax.broadcasted_iota(jnp.int32, (256, 256), 0) == low, 1.0, 0.0).astype(BF16)
        oh[:, pl.ds(off, 256)] = hot
        every = nn(xl[...], hot)
        vals = jnp.zeros((32, 256), F32)
        for h in range(16):
            vals = vals + jnp.where(high == h, every[h * 32 : (h + 1) * 32, :], 0.0)
        vals = vals.astype(BF16)
        gath[leaf] = vals
        skel = nt(vals, bases[leaf]).astype(BF16)
        rows = pl.ds(pl.multiple_of(leaf * 16, 16), 16)
        ag[0, rows, :] = skel[:16]
        ws[rows, :] = skel[16:]
        return xd + nt(skel[:16], trans[leaf]), wd + nn(skel[16:], trans[leaf])

    zero = jnp.zeros((16, 128), F32)
    xd, wd = lax.fori_loop(0, 16, leaf_in, (zero, zero))

    pl.semaphore_wait(barrier, 17)
    list_in = {}
    for i, d in enumerate((1, -1, 2, -2, 3, -3, 4)):
        origin = 4 if d == 4 else -d
        list_in[origin] = send(lists.at[0], lists.at[FPOS[origin]], list_s.at[i], list_r.at[i], z_dev(d))
    cw_in, cc_in = [], []

    def ag_cw(k):
        dst = 4 if k == 3 else -(k + 1)
        cw_in.append(send(ag.at[FPOS[-k]], ag.at[FPOS[dst]], ag_s.at[k], ag_r.at[k], z_dev(1)))

    def ag_cc(k):
        cc_in.append(send(ag.at[FPOS[k]], ag.at[FPOS[k + 1]], ag_s.at[4 + k], ag_r.at[4 + k], z_dev(-1)))

    ag_cw(0)
    ag_cc(0)

    loads[2].wait()
    loads[3].wait()
    xd2, wd2 = stacked(xd), stacked(wd)
    for v in range(6):
        cx = folded(nt(xd2, up[v]))
        cw = folded(nn(wd2, down[v]))
        lxs[0, v] = cx[:8]
        lxs[1, v] = cx[8:]
        lxs[2, v] = cw[:8]
        lxs[3, v] = cw[8:]
    lx_in = [
        send(lxs.at[lax.rem(b + d, 4)], lxr.at[d - 1], lx_s.at[d - 1], lx_r.at[d - 1], x_dev(d)) for d in range(1, 4)
    ]

    lane = lax.broadcasted_iota(jnp.int32, (16, 128), 1)
    spread = (
        (lax.broadcasted_iota(jnp.int32, (128, 256), 0) & 15) == (lax.broadcasted_iota(jnp.int32, (128, 256), 1) >> 4)
    ).astype(F32).astype(BF16)
    spread_t = (
        (lax.broadcasted_iota(jnp.int32, (256, 128), 1) & 15) == (lax.broadcasted_iota(jnp.int32, (256, 128), 0) >> 4)
    ).astype(F32)
    ones = jnp.ones((128, 256), BF16)

    def chosen(values, chunk):
        return jnp.where((lane >> 4) == chunk, values * 16.0, 0.0)

    def sum_matrix(values, chunk):
        line = nn(chosen(values, chunk).astype(BF16), spread)[:1]
        return jnp.where(diff_n[...] == line, 1.0, 0.0).astype(BF16)

    def pick_matrix(values, chunk):
        part = (spread_t * chosen(values, chunk)[:1]).astype(BF16)
        return jnp.where(diff_t[...] == nn(part, ones), 1.0, 0.0).astype(BF16)

    loads[4].wait()
    f_in, b_in = [], []

    def plane_send(buf_s, buf_r, lo, hi, sems_s, sems_r, k):
        copies = []
        for e in range(1, 8):
            copies.append(
                send(
                    buf_s.at[xor3(w, e), pl.ds(lo, hi - lo)],
                    buf_r.at[w, pl.ds(lo, hi - lo)],
                    sems_s.at[k, e - 1],
                    sems_r.at[k, e - 1],
                    w_dev(e),
                )
            )
        buf_r[w, lo:hi] = buf_s[w, lo:hi]
        return copies

    def ret_chunk(pos):
        chunk = lax.rem(z + BWD[pos] + 8, 8)
        picked = nn(pick_matrix(targets, chunk), ws[...]).astype(BF16).reshape(16, 16, 128)
        mats = coup[pl.ds(pl.multiple_of(chunk * 16, 16), 16)]
        ret = batch_nn(picked, mats).astype(BF16)
        bsend[:, pos] = ret.reshape(8, 32, 128)

    for k, (lo, hi) in enumerate(BBATCH):
        for pos in range(lo, hi):
            ret_chunk(pos)
        b_in.append(plane_send(bsend, brecv, lo, hi, b_s, b_r, k))

    def select(delta):
        pos = FPOS[delta]
        if delta:
            list_in[delta].wait_recv()
        picked = nn(pick_matrix(lists[pos].astype(F32), z), ag[pos]).astype(BF16)
        fsend[:, pos] = picked.reshape(8, 32, 128)

    def f_batch(k):
        lo, hi = FBATCH[k]
        for pos in range(lo, hi):
            select(FWD[pos])
        f_in.append(plane_send(fsend, frecv, lo, hi, f_s, f_r, k))

    def part(delta):
        values = lists[FPOS[delta]].astype(F32)
        return nn(sum_matrix(values, z), brecv[:, BPOS[delta]].reshape(256, 128))

    def wait_all(copies):
        for copy in copies:
            copy.wait_recv()

    rs_cw, rs_cc = [], []

    def rs_cw_send(k, value):
        cws[k] = value.astype(BF16)
        rs_cw.append(send(cws.at[k], cwr.at[k], cw_s.at[k], cw_r.at[k], z_dev(1)))

    def rs_cc_send(k, value):
        ccs[k] = value.astype(BF16)
        rs_cc.append(send(ccs.at[k], ccr.at[k], cc_s.at[k], cc_r.at[k], z_dev(-1)))

    def near_part(lo, hi):
        def body(leaf, carry):
            nterm[leaf, 0:16, :] = nt(gath[leaf, 0:16, :], near[leaf])
            nterm[leaf, 16:32, :] = nn(gath[leaf, 16:32, :], near[leaf])
            return carry

        lax.fori_loop(lo, hi, body, 0)

    def list_chunk(pos, total):
        chunk = lax.rem(z + FWD[pos] + 8, 8)
        inc = frecv[:, pos].reshape(16, 16, 128)
        mats = coup[pl.ds(pl.multiple_of(chunk * 16, 16), 16)]
        terms = batch_nt(inc, mats).reshape(256, 128)
        high, low = split(terms)
        both = nn(sum_matrix(targets, chunk), jnp.concatenate([high, low], axis=1))
        return total + both[:, :128] + both[:, 128:]

    cw_in[0].wait_recv()
    ag_cw(1)
    cc_in[0].wait_recv()
    ag_cc(1)
    f_batch(0)

    wait_all(lx_in)
    mine = lxs[b] + lxr[0] + lxr[1] + lxr[2]
    for v in range(3):
        lws[v, 0] = mine[v]
        lws[v, 1:4] = mine[3:6]
    lw_in = [
        send(lws.at[level_of(e)], lwr.at[e - 1], lw_s.at[e - 1], lw_r.at[e - 1], w_dev(e)) for e in range(1, 8)
    ]

    wait_all(b_in[0])
    list_in[4].wait_recv()
    rs_cc_send(0, part(4))
    wait_all(b_in[1])
    list_in[3].wait_recv()
    list_in[-3].wait_recv()
    rs_cw_send(0, part(3))
    loads[5].wait()
    near_part(0, 4)
    here = part(-3)
    rs_cc[0].wait_recv()
    rs_cc_send(1, here + ccr[0].astype(F32))

    cw_in[1].wait_recv()
    ag_cw(2)
    cc_in[1].wait_recv()
    ag_cc(2)
    list_in[2].wait_recv()
    list_in[-2].wait_recv()

    def f_batch_listed(k):
        lo, hi = FBATCH[k]
        for pos in range(lo, hi):
            picked = nn(pick_matrix(lists[pos].astype(F32), z), ag[pos]).astype(BF16)
            fsend[:, pos] = picked.reshape(8, 32, 128)
        f_in.append(plane_send(fsend, frecv, lo, hi, f_s, f_r, k))

    f_batch_listed(1)

    wait_all(lw_in)
    upper = mine[3:6]
    for e in range(1, 8):
        upper = upper + lwr[e - 1, 1:4]
    for v in range(3):
        lzs[v] = upper[v]
    lz_in = [send(lzs.at[level_of(e)], lzr.at[e - 1], lz_s.at[e - 1], lz_r.at[e - 1], zx_dev(e)) for e in range(1, 8)]

    wait_all(b_in[2])
    here_p, here_m = part(2), part(-2)
    rs_cw[0].wait_recv()
    rs_cw_send(1, here_p + cwr[0].astype(F32))
    rs_cc[1].wait_recv()
    rs_cc_send(2, here_m + ccr[1].astype(F32))
    near_part(4, 8)

    cw_in[2].wait_recv()
    ag_cw(3)
    cc_in[2].wait_recv()
    f_batch_listed(2)

    wait_all(lz_in)
    quarter = [
        lwr[0, 0],
        lwr[1, 0] + lwr[2, 0],
        lwr[3, 0] + lwr[4, 0] + lwr[5, 0] + lwr[6, 0],
        lzr[0],
        lzr[1] + lzr[2],
        lzr[3] + lzr[4] + lzr[5] + lzr[6],
    ]
    for v in range(6):
        lar[b, v] = quarter[v]
    la_in = [send(lar.at[b], lar.at[b], la_s.at[d - 1], la_r.at[d - 1], x_dev(d)) for d in range(1, 4)]

    wait_all(b_in[3])
    here_p, here_m, own = part(1), part(-1), part(0)
    rs_cw[1].wait_recv()
    rs_cw_send(2, here_p + cwr[1].astype(F32))
    rs_cc[2].wait_recv()
    rs_cc_send(3, here_m + ccr[2].astype(F32))

    near_part(8, 16)
    wait_all(f_in[0])
    lx = jnp.zeros((256, 128), F32)
    for pos in range(0, 3):
        lx = list_chunk(pos, lx)

    cw_in[3].wait_recv()
    f_batch_listed(3)

    for k in (1, 2):
        wait_all(f_in[k])
        for pos in range(*FBATCH[k]):
            lx = list_chunk(pos, lx)

    wait_all(la_in)
    yd = jnp.zeros((32, 128), F32)
    zd = jnp.zeros((32, 128), F32)
    for v in range(6):
        sx = jnp.concatenate([lar[0, v], lar[1, v]], axis=0)
        sw = jnp.concatenate([lar[2, v], lar[3, v]], axis=0)
        yd = yd + nt(stacked(sx), down[v])
        zd = zd + nn(stacked(sw), up[v])
    yd2, zd2 = stacked(folded(yd)), stacked(folded(zd))

    rs_cw[2].wait_recv()
    rs_cc[3].wait_recv()
    lw = own + cwr[2].astype(F32) + ccr[3].astype(F32)

    wait_all(f_in[3])
    lx = list_chunk(7, lx)

    acc[...] = jnp.zeros_like(acc)
    lsum = jnp.concatenate([lx.reshape(16, 16, 128), lw.reshape(16, 16, 128)], axis=1)


    for leaf in range(16):
        off = leaf * 256
        ys = folded(nn(yd2, trans[leaf]))
        zs = folded(nt(zd2, trans[leaf]))
        exp = (jnp.concatenate([ys, zs], axis=0) + lsum[leaf]).astype(BF16)
        vals = nn(exp, bases[leaf]) + nterm[leaf]
        high = pmap[:, off : off + 256] >> 8
        vals = vals.astype(BF16).astype(F32)
        masked = jnp.concatenate([jnp.where(high == h, vals, 0.0) for h in range(16)], axis=0).astype(BF16)
        acc[...] += nt(masked, oh[:, off : off + 256])

    for h in range(16):
        out_x[:, h * 256 : (h + 1) * 256] = acc[h * 32 : h * 32 + 16, :].astype(BF16)
        out_a[:, h * 256 : (h + 1) * 256] = acc[h * 32 + 16 : h * 32 + 32, :].astype(BF16)

    for copies in [list(list_in.values()), cw_in, cc_in, lx_in, lw_in, lz_in, la_in, rs_cw, rs_cc] + f_in + b_in:
        for copy in copies:
            copy.wait_send()


def shards(inputs, adjoint_in, panel_map, bases, near, trans, up, down, send_list, target_leaf, coup):
    vmem = pl.BlockSpec(memory_space=pltpu.VMEM)
    hbm = pl.BlockSpec(memory_space=pl.ANY)
    dma = pltpu.SemaphoreType.DMA
    return pl.pallas_call(
        kernel,
        out_shape=(jax.ShapeDtypeStruct((16, 4096), BF16), jax.ShapeDtypeStruct((16, 4096), BF16)),
        in_specs=[vmem] * 5 + [hbm] * 6,
        out_specs=(vmem, vmem),
        scratch_shapes=[
            pltpu.VMEM((16, 128, 256), BF16),
            pltpu.VMEM((16, 256, 256), BF16),
            pltpu.VMEM((16, 128, 128), BF16),
            pltpu.VMEM((6, 128, 128), BF16),
            pltpu.VMEM((6, 128, 128), BF16),
            pltpu.VMEM((128, 128, 128), BF16),
            pltpu.VMEM((512, 256), BF16),
            pltpu.VMEM((256, 4096), BF16),
            pltpu.VMEM((16, 32, 256), BF16),
            pltpu.VMEM((16, 32, 256), F32),
            pltpu.VMEM((256, 256), F32),
            pltpu.VMEM((256, 256), F32),
            pltpu.VMEM((512, 256), F32),
            pltpu.VMEM((8, 256, 128), BF16),
            pltpu.VMEM((256, 128), BF16),
            pltpu.VMEM((8, 16, 128), BF16),
            pltpu.VMEM((8, 8, 32, 128), BF16),
            pltpu.VMEM((8, 8, 32, 128), BF16),
            pltpu.VMEM((8, 8, 32, 128), BF16),
            pltpu.VMEM((8, 8, 32, 128), BF16),
            pltpu.VMEM((3, 256, 128), BF16),
            pltpu.VMEM((3, 256, 128), BF16),
            pltpu.VMEM((4, 256, 128), BF16),
            pltpu.VMEM((4, 256, 128), BF16),
            pltpu.VMEM((4, 6, 8, 128), F32),
            pltpu.VMEM((3, 6, 8, 128), F32),
            pltpu.VMEM((3, 4, 8, 128), F32),
            pltpu.VMEM((7, 4, 8, 128), F32),
            pltpu.VMEM((3, 8, 128), F32),
            pltpu.VMEM((7, 8, 128), F32),
            pltpu.VMEM((4, 6, 8, 128), F32),
            dma((6,)),
            dma((7,)), dma((7,)),
            dma((7,)), dma((7,)),
            dma((4, 7)), dma((4, 7)),
            dma((4, 7)), dma((4, 7)),
            dma((3,)), dma((3,)),
            dma((4,)), dma((4,)),
            dma((3,)), dma((3,)),
            dma((7,)), dma((7,)),
            dma((7,)), dma((7,)),
            dma((3,)), dma((3,)),
        ],
        compiler_params=pltpu.CompilerParams(
            collective_id=0, has_side_effects=True, vmem_limit_bytes=48 * 1024 * 1024
        ),
    )(inputs, adjoint_in, panel_map, send_list, target_leaf, bases, near, trans, up, down, coup)


def solution(mesh):
    each = ("sub", "blk")
    return jax.shard_map(
        shards,
        mesh=mesh,
        in_specs=(
            P(None, each),
            P(None, each),
            P(each, None),
            P(each, None, None),
            P(each, None, None),
            P(each, None, None),
            P(each, None, None),
            P(each, None, None),
            P(each, None),
            P(each, None),
            P(each, None, None),
        ),
        out_specs=(P(None, each), P(None, each)),
        check_vma=False,
    )
```

```python
import jax
import jax.numpy as jnp
from jax import lax
from jax.experimental import pallas as pl
from jax.experimental.pallas import tpu as pltpu
from jax.sharding import PartitionSpec as P

F32 = jnp.float32
BF16 = jnp.bfloat16
MESH = pl.DeviceIdType.MESH

FWD = (0, 1, -1, 2, -2, 3, -3, 4)
BWD = (4, 3, -3, 2, -2, 1, -1, 0)
FPOS = {d: i for i, d in enumerate(FWD)}
BPOS = {d: i for i, d in enumerate(BWD)}
FBATCH = ((0, 3), (3, 5), (5, 7), (7, 8))
BBATCH = ((0, 1), (1, 3), (3, 5), (5, 8))


def nt(a, b):
    return lax.dot_general(a, b, (((1,), (1,)), ((), ())), preferred_element_type=F32)


def nn(a, b):
    return lax.dot_general(a, b, (((1,), (0,)), ((), ())), preferred_element_type=F32)


def batch_nt(a, b):
    return lax.dot_general(a, b, (((2,), (2,)), ((0,), (0,))), preferred_element_type=F32)


def batch_nn(a, b):
    return lax.dot_general(a, b, (((2,), (1,)), ((0,), (0,))), preferred_element_type=F32)


def split(a):
    high = a.astype(BF16)
    low = (a - high.astype(F32)).astype(BF16)
    return high, low


def stacked(a):
    high, low = split(a)
    return jnp.concatenate([high, low], axis=0)


def folded(a):
    half = a.shape[0] // 2
    return a[:half] + a[half:]


def xor3(bits, e):
    total = 0
    for i in range(3):
        value = 1 - bits[i] if (e >> i) & 1 else bits[i]
        total = total + value * (1 << i)
    return total


def level_of(e):
    return 0 if e == 1 else (1 if e < 4 else 2)


def kernel(
    inp_h, adj_h, pmap_h, slist_h, tlist_h, bases_h, near_h, trans_h, up_h, down_h, coup_h,
    out_x, out_a,
    inp, adj, pmap, slist, tlist, bases, near, trans, up, down, coup,
    tsm, lsm,
    xl, oh, gath, nx, nw, diff_n, marked,
    ag0, ag1, ag2, ag3, ag4, ag5, ag6, ag7, ws, lists, fsend, frecv, bsend, brecv,
    cws, cwr, ccs, ccr,
    lxs, lxr, lws, lwr, lzs, lzr, lar,
    local_sem, ag_s, ag_r, list_s, list_r, f_s, f_r, b_s, b_r,
    cw_s, cw_r, cc_s, cc_r, lx_s, lx_r, lw_s, lw_r, lz_s, lz_r, la_s, la_r,
):
    ag = (ag0, ag1, ag2, ag3, ag4, ag5, ag6, ag7)
    s = lax.axis_index("sub")
    b = lax.axis_index("blk")

    loads = []

    def load(src, dst):
        copy = pltpu.make_async_copy(src, dst, local_sem.at[len(loads)])
        copy.start()
        loads.append(copy)
        return copy

    early = [load(inp_h, inp), load(adj_h, adj), load(pmap_h, pmap), load(slist_h, slist), load(tlist_h, tlist)]
    bases_in = load(bases_h, bases)
    trans_in = load(trans_h, trans)
    maps_in = [load(up_h, up), load(down_h, down)]
    tsm_in = load(tlist_h, tsm)
    coup_in = load(coup_h, coup)
    near_in = load(near_h, near)

    bits = []
    rest = s
    for _ in range(6):
        half = lax.div(rest, 2)
        bits.append(rest - half * 2)
        rest = half
    w = xor3(bits[:3], 0)
    z = xor3(bits[3:], 0)
    w_at = [xor3(bits[:3], e) for e in range(8)]
    zx_at = [xor3(bits[3:], e) for e in range(8)]
    z_at = {d: lax.rem(z + (d + 8), 8) for d in FWD}
    b_at = [lax.rem(b + d, 4) for d in range(4)]
    z_dev = {d: (z_at[d] * 8 + w, b) for d in FWD}
    zx_dev = [(zx_at[e] * 8 + w, b) for e in range(8)]
    w_dev = [(z * 8 + w_at[e], b) for e in range(8)]
    x_dev = [(s, b_at[d]) for d in range(4)]

    barrier = pltpu.get_barrier_semaphore()
    for e in range(1, 8):
        pl.semaphore_signal(barrier, inc=1, device_id=zx_dev[e], device_id_type=MESH)
        pl.semaphore_signal(barrier, inc=1, device_id=w_dev[e], device_id_type=MESH)
    for d in range(1, 4):
        pl.semaphore_signal(barrier, inc=1, device_id=x_dev[d], device_id_type=MESH)

    def send(src, dst, ssem, rsem, dev):
        copy = pltpu.make_async_remote_copy(
            src_ref=src, dst_ref=dst, send_sem=ssem, recv_sem=rsem, device_id=dev, device_id_type=MESH
        )
        copy.start()
        return copy

    def wait_all(copies):
        for copy in copies:
            copy.wait_recv()

    row = lax.broadcasted_iota(jnp.int32, (256, 256), 0)
    col = lax.broadcasted_iota(jnp.int32, (256, 256), 1)
    diff_n[...] = (row - (col & 15)).astype(F32)
    for copy in early:
        copy.wait()
    for h in range(16):
        xl[h * 32 : h * 32 + 16, :] = inp[:, h * 256 : (h + 1) * 256]
        xl[h * 32 + 16 : h * 32 + 32, :] = adj[:, h * 256 : (h + 1) * 256]
    lists[0] = jnp.broadcast_to(slist[...], (8, 128))

    def leaves_in(step, carry):
        for i in range(4):
            leaf = step * 4 + i
            off = pl.multiple_of(leaf * 256, 256)
            places = pmap[:, pl.ds(off, 256)]
            low, high = places & 255, places >> 8
            hot = jnp.where(lax.broadcasted_iota(jnp.int32, (256, 256), 0) == low, 1.0, 0.0).astype(BF16)
            oh[:, pl.ds(off, 256)] = hot
            every = nn(xl[...], hot)
            vals = jnp.zeros((32, 256), F32)
            for h in range(16):
                vals = vals + jnp.where(high == h, every[h * 32 : (h + 1) * 32, :], 0.0)
            gath[leaf] = vals.astype(BF16)
        return carry

    lax.fori_loop(0, 4, leaves_in, 0)
    bases_in.wait()
    skel = batch_nt(gath[...], bases[...]).astype(BF16)
    ag0[...] = skel[:, :16]
    ws[...] = skel[:, 16:]

    pl.semaphore_wait(barrier, 17)
    cw_in, cc_in = [], []

    def ag_cw(k):
        dst = 4 if k == 3 else -(k + 1)
        cw_in.append(send(ag[FPOS[-k]], ag[FPOS[dst]], ag_s.at[k], ag_r.at[k], z_dev[1]))

    def ag_cc(k):
        cc_in.append(send(ag[FPOS[k]], ag[FPOS[k + 1]], ag_s.at[4 + k], ag_r.at[4 + k], z_dev[-1]))

    ag_cw(0)
    ag_cc(0)
    list_in = []
    for i, d in enumerate((1, -1, 2, -2, 3, -3, 4)):
        origin = 4 if d == 4 else -d
        list_in.append(send(lists.at[0], lists.at[FPOS[origin]], list_s.at[i], list_r.at[i], z_dev[d]))

    trans_in.wait()
    xd = jnp.zeros((16, 128), F32)
    wd = jnp.zeros((16, 128), F32)
    for leaf in range(16):
        xd = xd + nt(skel[leaf, :16], trans[leaf])
        wd = wd + nn(skel[leaf, 16:], trans[leaf])
    for copy in maps_in:
        copy.wait()
    xd2, wd2 = stacked(xd), stacked(wd)
    for v in range(6):
        cx = folded(nt(xd2, up[v]))
        cw = folded(nn(wd2, down[v]))
        lxs[0, v] = cx[:8]
        lxs[1, v] = cx[8:]
        lxs[2, v] = cw[:8]
        lxs[3, v] = cw[8:]
    lx_in = [
        send(lxs.at[b_at[d]], lxr.at[d - 1], lx_s.at[d - 1], lx_r.at[d - 1], x_dev[d]) for d in range(1, 4)
    ]

    f_in, b_in = [], []

    def plane_send(buf_s, buf_r, lo, hi, sems_s, sems_r, k):
        copies = []
        for e in range(1, 8):
            copies.append(
                send(
                    buf_s.at[w_at[e], pl.ds(lo, hi - lo)],
                    buf_r.at[w, pl.ds(lo, hi - lo)],
                    sems_s.at[k, e - 1],
                    sems_r.at[k, e - 1],
                    w_dev[e],
                )
            )
        buf_r[w, lo:hi] = buf_s[w, lo:hi]
        return copies

    tsm_in.wait()
    coup_in.wait()

    def b_batch(k):
        lo, hi = BBATCH[k]
        for pos in range(lo, hi):
            first = z_at[BWD[pos]] * 16
            for i in range(16):
                ret = nn(ws[tsm[0, first + i]], coup[first + i]).astype(BF16)
                bsend[i // 2, pos, (i % 2) * 16 : (i % 2) * 16 + 16] = ret
        b_in.append(plane_send(bsend, brecv, lo, hi, b_s, b_r, k))

    b_batch(0)
    b_batch(1)

    lane = lax.broadcasted_iota(jnp.int32, (8, 128), 1)
    spread = (
        (lax.broadcasted_iota(jnp.int32, (128, 256), 0) & 15) == (lax.broadcasted_iota(jnp.int32, (128, 256), 1) >> 4)
    ).astype(F32).astype(BF16)
    turn = (lax.broadcasted_iota(jnp.int32, (8, 128), 0) + z) & 7
    t_rows = jnp.broadcast_to(tlist[...], (8, 128))
    t_line = nn(jnp.where((lane >> 4) == turn, t_rows * 16, 0).astype(F32).astype(BF16), spread)

    def sum_matrix(line):
        return jnp.where(diff_n[...] == line, 1.0, 0.0).astype(BF16)

    def select(pos):
        for i in range(16):
            leaf = lsm[pos, 0, z * 16 + i]
            fsend[i // 2, pos, (i % 2) * 16 : (i % 2) * 16 + 16] = ag[pos][leaf]

    def f_batch(k):
        lo, hi = FBATCH[k]
        for pos in range(lo, hi):
            select(pos)
        f_in.append(plane_send(fsend, frecv, lo, hi, f_s, f_r, k))

    rs_cw, rs_cc = [], []

    def rs_cw_send(k, value):
        cws[k] = value.astype(BF16)
        rs_cw.append(send(cws.at[k], cwr.at[k], cw_s.at[k], cw_r.at[k], z_dev[1]))

    def rs_cc_send(k, value):
        ccs[k] = value.astype(BF16)
        rs_cc.append(send(ccs.at[k], ccr.at[k], cc_s.at[k], cc_r.at[k], z_dev[-1]))

    def list_chunk(pos, total):
        delta = FWD[pos]
        inc = frecv[:, pos].reshape(16, 16, 128)
        mats = coup[pl.ds(pl.multiple_of(z_at[delta] * 16, 16), 16)]
        terms = batch_nt(inc, mats).reshape(256, 128)
        high, low = split(terms)
        r = delta % 8
        both = nn(sum_matrix(t_line[r : r + 1]), jnp.concatenate([high, low], axis=1))
        return total + both[:, :128] + both[:, 128:]

    cw_in[0].wait_recv()
    ag_cw(1)
    cc_in[0].wait_recv()
    ag_cc(1)
    wait_all(list_in)
    lists_in = load(lists, lsm)
    b_batch(2)

    l_line = nn(
        jnp.where((lane >> 4) == z, lists[:, 0, :] * 16, 0).astype(F32).astype(BF16), spread
    )

    def part(delta):
        pos = FPOS[delta]
        return nn(sum_matrix(l_line[pos : pos + 1]), brecv[:, BPOS[delta]].reshape(256, 128))

    wait_all(lx_in)
    mine = lxs[b] + lxr[0] + lxr[1] + lxr[2]
    for v in range(3):
        lws[v, 0] = mine[v]
        lws[v, 1:4] = mine[3:6]
    lw_in = [
        send(lws.at[level_of(e)], lwr.at[e - 1], lw_s.at[e - 1], lw_r.at[e - 1], w_dev[e]) for e in range(1, 8)
    ]

    lists_in.wait()
    f_batch(0)
    b_batch(3)

    wait_all(b_in[0])
    rs_cc_send(0, part(4))
    wait_all(b_in[1])
    rs_cw_send(0, part(3))
    here_m3 = part(-3)

    near_in.wait()
    nx[...] = batch_nt(gath[:, :16], near[...])

    cw_in[1].wait_recv()
    ag_cw(2)
    cc_in[1].wait_recv()
    ag_cc(2)
    f_batch(1)

    wait_all(lw_in)
    upper = mine[3:6]
    for e in range(1, 8):
        upper = upper + lwr[e - 1, 1:4]
    for v in range(3):
        lzs[v] = upper[v]
    lz_in = [send(lzs.at[level_of(e)], lzr.at[e - 1], lz_s.at[e - 1], lz_r.at[e - 1], zx_dev[e]) for e in range(1, 8)]

    wait_all(b_in[2])
    here_p, here_m = part(2), part(-2)
    rs_cc[0].wait_recv()
    rs_cc_send(1, here_m3 + ccr[0].astype(F32))
    rs_cw[0].wait_recv()
    rs_cw_send(1, here_p + cwr[0].astype(F32))

    nw[...] = batch_nn(gath[:, 16:], near[...])

    cw_in[2].wait_recv()
    ag_cw(3)
    cc_in[2].wait_recv()
    f_batch(2)

    wait_all(lz_in)
    quarter = [
        lwr[0, 0],
        lwr[1, 0] + lwr[2, 0],
        lwr[3, 0] + lwr[4, 0] + lwr[5, 0] + lwr[6, 0],
        lzr[0],
        lzr[1] + lzr[2],
        lzr[3] + lzr[4] + lzr[5] + lzr[6],
    ]
    for v in range(6):
        lar[b, v] = quarter[v]
    la_in = [send(lar.at[b], lar.at[b], la_s.at[d - 1], la_r.at[d - 1], x_dev[d]) for d in range(1, 4)]

    wait_all(b_in[3])
    here_p1, here_m1, own = part(1), part(-1), part(0)
    rs_cc[1].wait_recv()
    rs_cc_send(2, here_m + ccr[1].astype(F32))
    rs_cw[1].wait_recv()
    rs_cw_send(2, here_p1 + cwr[1].astype(F32))

    wait_all(f_in[0])
    lx = jnp.zeros((256, 128), F32)
    for pos in range(0, 3):
        lx = list_chunk(pos, lx)

    cw_in[3].wait_recv()
    f_batch(3)

    wait_all(la_in)
    yd = jnp.zeros((32, 128), F32)
    zd = jnp.zeros((32, 128), F32)
    for v in range(6):
        sx = jnp.concatenate([lar[0, v], lar[1, v]], axis=0)
        sw = jnp.concatenate([lar[2, v], lar[3, v]], axis=0)
        yd = yd + nt(stacked(sx), down[v])
        zd = zd + nn(stacked(sw), up[v])
    yd2, zd2 = stacked(folded(yd)), stacked(folded(zd))

    wait_all(f_in[1])
    for pos in range(3, 5):
        lx = list_chunk(pos, lx)

    rs_cc[2].wait_recv()
    rs_cc_send(3, here_m1 + ccr[2].astype(F32))

    wait_all(f_in[2])
    for pos in range(5, 7):
        lx = list_chunk(pos, lx)

    def expansions(value, from_lists, dot):
        rows = [folded(dot(value, trans[leaf])) for leaf in range(16)]
        return jnp.stack(rows, axis=0) + from_lists.reshape(16, 16, 128)

    def place(exp, near_term, out):
        vals = (batch_nn(exp.astype(BF16), bases[...]) + near_term[...]).astype(BF16).astype(F32)
        for leaf in range(16):
            high = pmap[:, leaf * 256 : (leaf + 1) * 256] >> 8
            marked[:, leaf * 256 : (leaf + 1) * 256] = jnp.concatenate(
                [jnp.where(high == h, vals[leaf], 0.0) for h in range(16)], axis=0
            ).astype(BF16)
        res = nt(marked[...], oh[...]).astype(BF16)
        for h in range(16):
            out[:, h * 256 : (h + 1) * 256] = res[h * 16 : h * 16 + 16]

    wait_all(f_in[3])
    lx = list_chunk(7, lx)
    place(expansions(yd2, lx, nn), nx, out_x)

    rs_cw[2].wait_recv()
    rs_cc[3].wait_recv()
    lw = own + cwr[2].astype(F32) + ccr[3].astype(F32)
    place(expansions(zd2, lw, nt), nw, out_a)

    for copies in [list_in, cw_in, cc_in, lx_in, lw_in, lz_in, la_in, rs_cw, rs_cc] + f_in + b_in:
        for copy in copies:
            copy.wait_send()


def hand_over(x_ref, a_ref, out_x, out_a):
    out_x[...] = x_ref[...]
    out_a[...] = a_ref[...]


def shards(inputs, adjoint_in, panel_map, bases, near, trans, up, down, send_list, target_leaf, coup):
    vmem = pl.BlockSpec(memory_space=pltpu.VMEM)
    hbm = pl.BlockSpec(memory_space=pltpu.HBM)
    dma = pltpu.SemaphoreType.DMA
    both = pl.pallas_call(
        kernel,
        out_shape=(jax.ShapeDtypeStruct((16, 4096), BF16), jax.ShapeDtypeStruct((16, 4096), BF16)),
        in_specs=[hbm] * 11,
        out_specs=(vmem, vmem),
        scratch_shapes=[
            pltpu.VMEM((16, 4096), BF16),
            pltpu.VMEM((16, 4096), BF16),
            pltpu.VMEM((1, 4096), jnp.int32),
            pltpu.VMEM((1, 128), jnp.int32),
            pltpu.VMEM((1, 128), jnp.int32),
            pltpu.VMEM((16, 128, 256), BF16),
            pltpu.VMEM((16, 256, 256), BF16),
            pltpu.VMEM((16, 128, 128), BF16),
            pltpu.VMEM((6, 128, 128), BF16),
            pltpu.VMEM((6, 128, 128), BF16),
            pltpu.VMEM((128, 128, 128), BF16),
            pltpu.SMEM((1, 128), jnp.int32),
            pltpu.SMEM((8, 8, 128), jnp.int32),
            pltpu.VMEM((512, 256), BF16),
            pltpu.VMEM((256, 4096), BF16),
            pltpu.VMEM((16, 32, 256), BF16),
            pltpu.VMEM((16, 16, 256), F32),
            pltpu.VMEM((16, 16, 256), F32),
            pltpu.VMEM((256, 256), F32),
            pltpu.VMEM((256, 4096), BF16),
        ]
        + [pltpu.VMEM((16, 16, 128), BF16)] * 8
        + [
            pltpu.VMEM((16, 16, 128), BF16),
            pltpu.VMEM((8, 8, 128), jnp.int32),
            pltpu.VMEM((8, 8, 32, 128), BF16),
            pltpu.VMEM((8, 8, 32, 128), BF16),
            pltpu.VMEM((8, 8, 32, 128), BF16),
            pltpu.VMEM((8, 8, 32, 128), BF16),
            pltpu.VMEM((3, 256, 128), BF16),
            pltpu.VMEM((3, 256, 128), BF16),
            pltpu.VMEM((4, 256, 128), BF16),
            pltpu.VMEM((4, 256, 128), BF16),
            pltpu.VMEM((4, 6, 8, 128), F32),
            pltpu.VMEM((3, 6, 8, 128), F32),
            pltpu.VMEM((3, 4, 8, 128), F32),
            pltpu.VMEM((7, 4, 8, 128), F32),
            pltpu.VMEM((3, 8, 128), F32),
            pltpu.VMEM((7, 8, 128), F32),
            pltpu.VMEM((4, 6, 8, 128), F32),
            dma((13,)),
            dma((7,)), dma((7,)),
            dma((7,)), dma((7,)),
            dma((4, 7)), dma((4, 7)),
            dma((4, 7)), dma((4, 7)),
            dma((3,)), dma((3,)),
            dma((4,)), dma((4,)),
            dma((3,)), dma((3,)),
            dma((7,)), dma((7,)),
            dma((7,)), dma((7,)),
            dma((3,)), dma((3,)),
        ],
        compiler_params=pltpu.CompilerParams(
            collective_id=0, has_side_effects=True, vmem_limit_bytes=60 * 1024 * 1024
        ),
    )(inputs, adjoint_in, panel_map, send_list, target_leaf, bases, near, trans, up, down, coup)
    shape = jax.ShapeDtypeStruct((16, 4096), BF16)
    return pl.pallas_call(hand_over, out_shape=(shape, shape), in_specs=[vmem] * 2, out_specs=(vmem, vmem))(*both)


def solution(mesh):
    each = ("sub", "blk")
    return jax.shard_map(
        shards,
        mesh=mesh,
        in_specs=(
            P(None, each),
            P(None, each),
            P(each, None),
            P(each, None, None),
            P(each, None, None),
            P(each, None, None),
            P(each, None, None),
            P(each, None, None),
            P(each, None),
            P(each, None),
            P(each, None, None),
        ),
        out_specs=(P(None, each), P(None, each)),
        check_vma=False,
    )
```

```python
import jax
import jax.numpy as jnp
from jax import lax
from jax.experimental import pallas as pl
from jax.experimental.pallas import tpu as pltpu
from jax.sharding import PartitionSpec as P

F32 = jnp.float32
BF16 = jnp.bfloat16
MESH = pl.DeviceIdType.MESH

FWD = (0, 1, -1, 2, -2, 3, -3, 4)
BWD = (4, 3, -3, 2, -2, 1, -1, 0)
FPOS = {d: i for i, d in enumerate(FWD)}
BPOS = {d: i for i, d in enumerate(BWD)}
FBATCH = ((0, 3), (3, 7), (7, 8))
BBATCH = ((0, 1), (1, 3), (3, 5), (5, 8))


def nt(a, b):
    return lax.dot_general(a, b, (((1,), (1,)), ((), ())), preferred_element_type=F32)


def nn(a, b):
    return lax.dot_general(a, b, (((1,), (0,)), ((), ())), preferred_element_type=F32)


def batch_nt(a, b):
    return lax.dot_general(a, b, (((2,), (2,)), ((0,), (0,))), preferred_element_type=F32)


def batch_nn(a, b):
    return lax.dot_general(a, b, (((2,), (1,)), ((0,), (0,))), preferred_element_type=F32)


def split(a):
    high = a.astype(BF16)
    low = (a - high.astype(F32)).astype(BF16)
    return high, low


def stacked(a):
    high, low = split(a)
    return jnp.concatenate([high, low], axis=0)


def folded(a):
    half = a.shape[0] // 2
    return a[:half] + a[half:]


def xor3(bits, e):
    total = 0
    for i in range(3):
        value = 1 - bits[i] if (e >> i) & 1 else bits[i]
        total = total + value * (1 << i)
    return total


def level_of(e):
    return 0 if e == 1 else (1 if e < 4 else 2)


def kernel(
    inp_h, adj_h, pmap_h, slist_h, tlist_h, bases_h, near_h, trans_h, up_h, down_h, coup_h,
    out_x, out_a,
    inp, adj, pmap, slist, tlist, bases, near, trans, up, down, coup,
    tsm, lsm,
    xl, oh, oh_t, gath, nx, nw, diff_n, marked,
    ag0, ag1, ag2, ag3, ag4, ag5, ag6, ag7, ws, lists, fsend, frecv, bsend, brecv,
    cws, cwr, ccs, ccr,
    lxs, lxr, lws, lwr, lzs, lzr, lar,
    local_sem, ag_s, ag_r, list_s, list_r, f_s, f_r, b_s, b_r,
    cw_s, cw_r, cc_s, cc_r, lx_s, lx_r, lw_s, lw_r, lz_s, lz_r, la_s, la_r,
):
    ag = (ag0, ag1, ag2, ag3, ag4, ag5, ag6, ag7)
    s = lax.axis_index("sub")
    b = lax.axis_index("blk")

    loads = []

    def load(src, dst):
        copy = pltpu.make_async_copy(src, dst, local_sem.at[len(loads)])
        copy.start()
        loads.append(copy)
        return copy

    early = [load(inp_h, inp), load(adj_h, adj), load(pmap_h, pmap), load(slist_h, slist), load(tlist_h, tlist)]
    bases_in = load(bases_h, bases)
    trans_in = load(trans_h, trans)
    maps_in = [load(up_h, up), load(down_h, down)]
    tsm_in = load(tlist_h, tsm)
    coup_in = load(coup_h, coup)
    near_in = load(near_h, near)

    bits = []
    rest = s
    for _ in range(6):
        half = lax.div(rest, 2)
        bits.append(rest - half * 2)
        rest = half
    w = xor3(bits[:3], 0)
    z = xor3(bits[3:], 0)
    w_at = [xor3(bits[:3], e) for e in range(8)]
    zx_at = [xor3(bits[3:], e) for e in range(8)]
    z_at = {d: lax.rem(z + (d + 8), 8) for d in FWD}
    b_at = [lax.rem(b + d, 4) for d in range(4)]
    z_dev = {d: (z_at[d] * 8 + w, b) for d in FWD}
    zx_dev = [(zx_at[e] * 8 + w, b) for e in range(8)]
    w_dev = [(z * 8 + w_at[e], b) for e in range(8)]
    x_dev = [(s, b_at[d]) for d in range(4)]

    barrier = pltpu.get_barrier_semaphore()
    for e in range(1, 8):
        pl.semaphore_signal(barrier, inc=1, device_id=zx_dev[e], device_id_type=MESH)
        pl.semaphore_signal(barrier, inc=1, device_id=w_dev[e], device_id_type=MESH)
    for d in range(1, 4):
        pl.semaphore_signal(barrier, inc=1, device_id=x_dev[d], device_id_type=MESH)

    def send(src, dst, ssem, rsem, dev):
        copy = pltpu.make_async_remote_copy(
            src_ref=src, dst_ref=dst, send_sem=ssem, recv_sem=rsem, device_id=dev, device_id_type=MESH
        )
        copy.start()
        return copy

    def wait_all(copies):
        for copy in copies:
            copy.wait_recv()

    row = lax.broadcasted_iota(jnp.int32, (256, 256), 0)
    col = lax.broadcasted_iota(jnp.int32, (256, 256), 1)
    diff_n[...] = (row - (col & 15)).astype(F32)
    for copy in early:
        copy.wait()
    for h in range(16):
        xl[h * 32 : h * 32 + 16, :] = inp[:, h * 256 : (h + 1) * 256]
        xl[h * 32 + 16 : h * 32 + 32, :] = adj[:, h * 256 : (h + 1) * 256]
    lists[0] = jnp.broadcast_to(slist[...], (8, 128))

    def leaves_in(step, carry):
        for i in range(4):
            leaf = step * 4 + i
            off = pl.multiple_of(leaf * 256, 256)
            places = pmap[:, pl.ds(off, 256)]
            low, high = places & 255, places >> 8
            hot = jnp.where(lax.broadcasted_iota(jnp.int32, (256, 256), 0) == low, 1.0, 0.0).astype(BF16)
            oh[:, pl.ds(off, 256)] = hot
            every = nn(xl[...], hot)
            vals = jnp.zeros((32, 256), F32)
            for h in range(16):
                vals = vals + jnp.where(high == h, every[h * 32 : (h + 1) * 32, :], 0.0)
            gath[leaf] = vals.astype(BF16)
        return carry

    lax.fori_loop(0, 4, leaves_in, 0)
    bases_in.wait()
    skel = batch_nt(gath[...], bases[...]).astype(BF16)
    ag0[...] = skel[:, :16]
    ws[...] = skel[:, 16:]

    pl.semaphore_wait(barrier, 17)
    cw_in, cc_in = [], []

    def ag_cw(k):
        dst = 4 if k == 3 else -(k + 1)
        cw_in.append(send(ag[FPOS[-k]], ag[FPOS[dst]], ag_s.at[k], ag_r.at[k], z_dev[1]))

    def ag_cc(k):
        cc_in.append(send(ag[FPOS[k]], ag[FPOS[k + 1]], ag_s.at[4 + k], ag_r.at[4 + k], z_dev[-1]))

    ag_cw(0)
    ag_cc(0)
    list_in = []
    for i, d in enumerate((1, -1, 2, -2, 3, -3, 4)):
        origin = 4 if d == 4 else -d
        list_in.append(send(lists.at[0], lists.at[FPOS[origin]], list_s.at[i], list_r.at[i], z_dev[d]))

    trans_in.wait()
    xd = jnp.zeros((16, 128), F32)
    wd = jnp.zeros((16, 128), F32)
    for leaf in range(16):
        xd = xd + nt(skel[leaf, :16], trans[leaf])
        wd = wd + nn(skel[leaf, 16:], trans[leaf])
    for copy in maps_in:
        copy.wait()
    xd2, wd2 = stacked(xd), stacked(wd)
    for v in range(6):
        cx = folded(nt(xd2, up[v]))
        cw = folded(nn(wd2, down[v]))
        lxs[0, v] = cx[:8]
        lxs[1, v] = cx[8:]
        lxs[2, v] = cw[:8]
        lxs[3, v] = cw[8:]
    lx_in = [
        send(lxs.at[b_at[d]], lxr.at[d - 1], lx_s.at[d - 1], lx_r.at[d - 1], x_dev[d]) for d in range(1, 4)
    ]

    f_in, b_in = [], []

    def plane_send(buf_s, buf_r, lo, hi, sems_s, sems_r, k):
        copies = []
        for e in range(1, 8):
            copies.append(
                send(
                    buf_s.at[w_at[e], pl.ds(lo, hi - lo)],
                    buf_r.at[w, pl.ds(lo, hi - lo)],
                    sems_s.at[k, e - 1],
                    sems_r.at[k, e - 1],
                    w_dev[e],
                )
            )
        buf_r[w, lo:hi] = buf_s[w, lo:hi]
        return copies

    tsm_in.wait()
    coup_in.wait()

    def b_batch(k):
        lo, hi = BBATCH[k]
        for pos in range(lo, hi):
            first = z_at[BWD[pos]] * 16
            for i in range(16):
                ret = nn(ws[tsm[0, first + i]], coup[first + i]).astype(BF16)
                bsend[i // 2, pos, (i % 2) * 16 : (i % 2) * 16 + 16] = ret
        b_in.append(plane_send(bsend, brecv, lo, hi, b_s, b_r, k))

    b_batch(0)
    b_batch(1)

    lane = lax.broadcasted_iota(jnp.int32, (8, 128), 1)
    spread = (
        (lax.broadcasted_iota(jnp.int32, (128, 256), 0) & 15) == (lax.broadcasted_iota(jnp.int32, (128, 256), 1) >> 4)
    ).astype(F32).astype(BF16)
    turn = (lax.broadcasted_iota(jnp.int32, (8, 128), 0) + z) & 7
    t_rows = jnp.broadcast_to(tlist[...], (8, 128))
    t_line = nn(jnp.where((lane >> 4) == turn, t_rows * 16, 0).astype(F32).astype(BF16), spread)

    def sum_matrix(line):
        return jnp.where(diff_n[...] == line, 1.0, 0.0).astype(BF16)

    def select(pos):
        for i in range(16):
            leaf = lsm[pos, 0, z * 16 + i]
            fsend[i // 2, pos, (i % 2) * 16 : (i % 2) * 16 + 16] = ag[pos][leaf]

    def f_batch(k):
        lo, hi = FBATCH[k]
        for pos in range(lo, hi):
            select(pos)
        f_in.append(plane_send(fsend, frecv, lo, hi, f_s, f_r, k))

    rs_cw, rs_cc = [], []

    def rs_cw_send(k, value):
        cws[k] = value.astype(BF16)
        rs_cw.append(send(cws.at[k], cwr.at[k], cw_s.at[k], cw_r.at[k], z_dev[1]))

    def rs_cc_send(k, value):
        ccs[k] = value.astype(BF16)
        rs_cc.append(send(ccs.at[k], ccr.at[k], cc_s.at[k], cc_r.at[k], z_dev[-1]))

    def list_chunk(pos, total):
        delta = FWD[pos]
        inc = frecv[:, pos].reshape(16, 16, 128)
        mats = coup[pl.ds(pl.multiple_of(z_at[delta] * 16, 16), 16)]
        terms = batch_nt(inc, mats).reshape(256, 128)
        high, low = split(terms)
        r = delta % 8
        both = nn(sum_matrix(t_line[r : r + 1]), jnp.concatenate([high, low], axis=1))
        return total + both[:, :128] + both[:, 128:]

    cw_in[0].wait_recv()
    ag_cw(1)
    cc_in[0].wait_recv()
    ag_cc(1)
    wait_all(list_in)
    lists_in = load(lists, lsm)
    b_batch(2)

    l_line = nn(
        jnp.where((lane >> 4) == z, lists[:, 0, :] * 16, 0).astype(F32).astype(BF16), spread
    )

    def part(delta):
        pos = FPOS[delta]
        return nn(sum_matrix(l_line[pos : pos + 1]), brecv[:, BPOS[delta]].reshape(256, 128))

    wait_all(lx_in)
    mine = lxs[b] + lxr[0] + lxr[1] + lxr[2]
    for v in range(3):
        lws[v, 0] = mine[v]
        lws[v, 1:4] = mine[3:6]
    lw_in = [
        send(lws.at[level_of(e)], lwr.at[e - 1], lw_s.at[e - 1], lw_r.at[e - 1], w_dev[e]) for e in range(1, 8)
    ]

    lists_in.wait()
    f_batch(0)
    b_batch(3)

    wait_all(b_in[0])
    rs_cc_send(0, part(4))
    wait_all(b_in[1])
    rs_cw_send(0, part(3))
    here_m3 = part(-3)

    near_in.wait()
    nx[...] = batch_nt(gath[:, :16], near[...])

    cw_in[1].wait_recv()
    ag_cw(2)
    cc_in[1].wait_recv()
    ag_cc(2)

    wait_all(lw_in)
    upper = mine[3:6]
    for e in range(1, 8):
        upper = upper + lwr[e - 1, 1:4]
    for v in range(3):
        lzs[v] = upper[v]
    lz_in = [send(lzs.at[level_of(e)], lzr.at[e - 1], lz_s.at[e - 1], lz_r.at[e - 1], zx_dev[e]) for e in range(1, 8)]

    wait_all(b_in[2])
    here_p, here_m = part(2), part(-2)
    rs_cc[0].wait_recv()
    rs_cc_send(1, here_m3 + ccr[0].astype(F32))
    rs_cw[0].wait_recv()
    rs_cw_send(1, here_p + cwr[0].astype(F32))

    nw[...] = batch_nn(gath[:, 16:], near[...])
    unit = jnp.where(row == col, 1.0, 0.0).astype(BF16)
    for leaf in range(16):
        oh_t[leaf * 256 : (leaf + 1) * 256, :] = lax.dot_general(
            oh[:, leaf * 256 : (leaf + 1) * 256], unit, (((0,), (0,)), ((), ())), preferred_element_type=F32
        ).astype(BF16)

    cw_in[2].wait_recv()
    ag_cw(3)
    cc_in[2].wait_recv()
    f_batch(1)

    wait_all(lz_in)
    quarter = [
        lwr[0, 0],
        lwr[1, 0] + lwr[2, 0],
        lwr[3, 0] + lwr[4, 0] + lwr[5, 0] + lwr[6, 0],
        lzr[0],
        lzr[1] + lzr[2],
        lzr[3] + lzr[4] + lzr[5] + lzr[6],
    ]
    for v in range(6):
        lar[b, v] = quarter[v]
    la_in = [send(lar.at[b], lar.at[b], la_s.at[d - 1], la_r.at[d - 1], x_dev[d]) for d in range(1, 4)]

    wait_all(b_in[3])
    here_p1, here_m1, own = part(1), part(-1), part(0)
    rs_cc[1].wait_recv()
    rs_cc_send(2, here_m + ccr[1].astype(F32))
    rs_cw[1].wait_recv()
    rs_cw_send(2, here_p1 + cwr[1].astype(F32))

    wait_all(f_in[0])
    lx = jnp.zeros((256, 128), F32)
    for pos in range(0, 3):
        lx = list_chunk(pos, lx)

    cw_in[3].wait_recv()
    f_batch(2)

    wait_all(la_in)
    yd = jnp.zeros((32, 128), F32)
    zd = jnp.zeros((32, 128), F32)
    for v in range(6):
        sx = jnp.concatenate([lar[0, v], lar[1, v]], axis=0)
        sw = jnp.concatenate([lar[2, v], lar[3, v]], axis=0)
        yd = yd + nt(stacked(sx), down[v])
        zd = zd + nn(stacked(sw), up[v])
    yd2, zd2 = stacked(folded(yd)), stacked(folded(zd))
    y_leaf = jnp.stack([folded(nn(yd2, trans[leaf])) for leaf in range(16)], axis=0)
    z_leaf = jnp.stack([folded(nt(zd2, trans[leaf])) for leaf in range(16)], axis=0)

    wait_all(f_in[1])
    for pos in range(3, 5):
        lx = list_chunk(pos, lx)

    rs_cc[2].wait_recv()
    rs_cc_send(3, here_m1 + ccr[2].astype(F32))

    for pos in range(5, 7):
        lx = list_chunk(pos, lx)

    def place(exp, near_term, out):
        vals = (batch_nn(exp.astype(BF16), bases[...]) + near_term[...]).astype(BF16).astype(F32)
        for leaf in range(16):
            high = pmap[:, leaf * 256 : (leaf + 1) * 256] >> 8
            marked[:, leaf * 256 : (leaf + 1) * 256] = jnp.concatenate(
                [jnp.where(high == h, vals[leaf], 0.0) for h in range(16)], axis=0
            ).astype(BF16)
        res = nn(marked[...], oh_t[...]).astype(BF16)
        for h in range(16):
            out[:, h * 256 : (h + 1) * 256] = res[h * 16 : h * 16 + 16]

    wait_all(f_in[2])
    lx = list_chunk(7, lx)
    place(y_leaf + lx.reshape(16, 16, 128), nx, out_x)

    rs_cw[2].wait_recv()
    rs_cc[3].wait_recv()
    lw = own + cwr[2].astype(F32) + ccr[3].astype(F32)
    place(z_leaf + lw.reshape(16, 16, 128), nw, out_a)

    for copies in [list_in, cw_in, cc_in, lx_in, lw_in, lz_in, la_in, rs_cw, rs_cc] + f_in + b_in:
        for copy in copies:
            copy.wait_send()


def hand_over(x_ref, a_ref, out_x, out_a):
    out_x[...] = x_ref[...]
    out_a[...] = a_ref[...]


def shards(inputs, adjoint_in, panel_map, bases, near, trans, up, down, send_list, target_leaf, coup):
    vmem = pl.BlockSpec(memory_space=pltpu.VMEM)
    hbm = pl.BlockSpec(memory_space=pltpu.HBM)
    dma = pltpu.SemaphoreType.DMA
    both = pl.pallas_call(
        kernel,
        out_shape=(jax.ShapeDtypeStruct((16, 4096), BF16), jax.ShapeDtypeStruct((16, 4096), BF16)),
        in_specs=[hbm] * 11,
        out_specs=(vmem, vmem),
        scratch_shapes=[
            pltpu.VMEM((16, 4096), BF16),
            pltpu.VMEM((16, 4096), BF16),
            pltpu.VMEM((1, 4096), jnp.int32),
            pltpu.VMEM((1, 128), jnp.int32),
            pltpu.VMEM((1, 128), jnp.int32),
            pltpu.VMEM((16, 128, 256), BF16),
            pltpu.VMEM((16, 256, 256), BF16),
            pltpu.VMEM((16, 128, 128), BF16),
            pltpu.VMEM((6, 128, 128), BF16),
            pltpu.VMEM((6, 128, 128), BF16),
            pltpu.VMEM((128, 128, 128), BF16),
            pltpu.SMEM((1, 128), jnp.int32),
            pltpu.SMEM((8, 8, 128), jnp.int32),
            pltpu.VMEM((512, 256), BF16),
            pltpu.VMEM((256, 4096), BF16),
            pltpu.VMEM((4096, 256), BF16),
            pltpu.VMEM((16, 32, 256), BF16),
            pltpu.VMEM((16, 16, 256), F32),
            pltpu.VMEM((16, 16, 256), F32),
            pltpu.VMEM((256, 256), F32),
            pltpu.VMEM((256, 4096), BF16),
        ]
        + [pltpu.VMEM((16, 16, 128), BF16)] * 8
        + [
            pltpu.VMEM((16, 16, 128), BF16),
            pltpu.VMEM((8, 8, 128), jnp.int32),
            pltpu.VMEM((8, 8, 32, 128), BF16),
            pltpu.VMEM((8, 8, 32, 128), BF16),
            pltpu.VMEM((8, 8, 32, 128), BF16),
            pltpu.VMEM((8, 8, 32, 128), BF16),
            pltpu.VMEM((3, 256, 128), BF16),
            pltpu.VMEM((3, 256, 128), BF16),
            pltpu.VMEM((4, 256, 128), BF16),
            pltpu.VMEM((4, 256, 128), BF16),
            pltpu.VMEM((4, 6, 8, 128), F32),
            pltpu.VMEM((3, 6, 8, 128), F32),
            pltpu.VMEM((3, 4, 8, 128), F32),
            pltpu.VMEM((7, 4, 8, 128), F32),
            pltpu.VMEM((3, 8, 128), F32),
            pltpu.VMEM((7, 8, 128), F32),
            pltpu.VMEM((4, 6, 8, 128), F32),
            dma((13,)),
            dma((7,)), dma((7,)),
            dma((7,)), dma((7,)),
            dma((4, 7)), dma((4, 7)),
            dma((4, 7)), dma((4, 7)),
            dma((3,)), dma((3,)),
            dma((4,)), dma((4,)),
            dma((3,)), dma((3,)),
            dma((7,)), dma((7,)),
            dma((7,)), dma((7,)),
            dma((3,)), dma((3,)),
        ],
        compiler_params=pltpu.CompilerParams(
            collective_id=0, has_side_effects=True, vmem_limit_bytes=60 * 1024 * 1024
        ),
    )(inputs, adjoint_in, panel_map, send_list, target_leaf, bases, near, trans, up, down, coup)
    shape = jax.ShapeDtypeStruct((16, 4096), BF16)
    return pl.pallas_call(hand_over, out_shape=(shape, shape), in_specs=[vmem] * 2, out_specs=(vmem, vmem))(*both)


def solution(mesh):
    each = ("sub", "blk")
    return jax.shard_map(
        shards,
        mesh=mesh,
        in_specs=(
            P(None, each),
            P(None, each),
            P(each, None),
            P(each, None, None),
            P(each, None, None),
            P(each, None, None),
            P(each, None, None),
            P(each, None, None),
            P(each, None),
            P(each, None),
            P(each, None, None),
        ),
        out_specs=(P(None, each), P(None, each)),
        check_vma=False,
    )
```

```python
import jax
import jax.numpy as jnp
from jax import lax
from jax.experimental import pallas as pl
from jax.experimental.pallas import tpu as pltpu
from jax.sharding import PartitionSpec as P

F32 = jnp.float32
BF16 = jnp.bfloat16
MESH = pl.DeviceIdType.MESH

FWD = (0, 1, -1, 2, -2, 3, -3, 4)
BWD = (4, 3, -3, 2, -2, 1, -1, 0)
FPOS = {d: i for i, d in enumerate(FWD)}
BPOS = {d: i for i, d in enumerate(BWD)}
FBATCH = ((0, 3), (3, 7), (7, 8))
BBATCH = ((0, 1), (1, 3), (3, 5), (5, 8))


def nt(a, b):
    return lax.dot_general(a, b, (((1,), (1,)), ((), ())), preferred_element_type=F32)


def nn(a, b):
    return lax.dot_general(a, b, (((1,), (0,)), ((), ())), preferred_element_type=F32)


def batch_nt(a, b):
    return lax.dot_general(a, b, (((2,), (2,)), ((0,), (0,))), preferred_element_type=F32)


def batch_nn(a, b):
    return lax.dot_general(a, b, (((2,), (1,)), ((0,), (0,))), preferred_element_type=F32)


def split(a):
    high = a.astype(BF16)
    low = (a - high.astype(F32)).astype(BF16)
    return high, low


def stacked(a):
    high, low = split(a)
    return jnp.concatenate([high, low], axis=0)


def folded(a):
    half = a.shape[0] // 2
    return a[:half] + a[half:]


def xor3(bits, e):
    total = 0
    for i in range(3):
        value = 1 - bits[i] if (e >> i) & 1 else bits[i]
        total = total + value * (1 << i)
    return total


def level_of(e):
    return 0 if e == 1 else (1 if e < 4 else 2)


def kernel(
    inp_h, adj_h, pmap_h, slist_h, tlist_h, bases_h, near_h, trans_h, up_h, down_h, coup_h,
    out_x, out_a,
    inp, adj, pmap, slist, tlist, bases, near, trans, up, down, coup,
    tsm, lsm,
    xl, oh, oh_t, gath, nx, nw, diff_n, marked,
    ag0, ag1, ag2, ag3, ag4, ag5, ag6, ag7, ws, lists, fsend, frecv, bsend, brecv,
    cws, cwr, ccs, ccr,
    lxs, lxr, lws, lwr, lzs, lzr, lar,
    local_sem, ag_s, ag_r, list_s, list_r, f_s, f_r, b_s, b_r,
    cw_s, cw_r, cc_s, cc_r, lx_s, lx_r, lw_s, lw_r, lz_s, lz_r, la_s, la_r,
):
    ag = (ag0, ag1, ag2, ag3, ag4, ag5, ag6, ag7)
    s = lax.axis_index("sub")
    b = lax.axis_index("blk")

    loads = []

    def load(src, dst):
        copy = pltpu.make_async_copy(src, dst, local_sem.at[len(loads)])
        copy.start()
        loads.append(copy)
        return copy

    early = [load(inp_h, inp), load(adj_h, adj), load(pmap_h, pmap), load(slist_h, slist), load(tlist_h, tlist)]
    bases_in = load(bases_h, bases)
    trans_in = load(trans_h, trans)
    maps_in = [load(up_h, up), load(down_h, down)]
    tsm_in = load(tlist_h, tsm)

    bits = []
    rest = s
    for _ in range(6):
        half = lax.div(rest, 2)
        bits.append(rest - half * 2)
        rest = half
    w = xor3(bits[:3], 0)
    z = xor3(bits[3:], 0)
    w_at = [xor3(bits[:3], e) for e in range(8)]
    zx_at = [xor3(bits[3:], e) for e in range(8)]
    z_at = {d: lax.rem(z + (d + 8), 8) for d in FWD}
    b_at = [lax.rem(b + d, 4) for d in range(4)]
    z_dev = {d: (z_at[d] * 8 + w, b) for d in FWD}
    zx_dev = [(zx_at[e] * 8 + w, b) for e in range(8)]
    w_dev = [(z * 8 + w_at[e], b) for e in range(8)]
    x_dev = [(s, b_at[d]) for d in range(4)]

    barrier = pltpu.get_barrier_semaphore()
    for e in range(1, 8):
        pl.semaphore_signal(barrier, inc=1, device_id=zx_dev[e], device_id_type=MESH)
        pl.semaphore_signal(barrier, inc=1, device_id=w_dev[e], device_id_type=MESH)
    for d in range(1, 4):
        pl.semaphore_signal(barrier, inc=1, device_id=x_dev[d], device_id_type=MESH)

    def send(src, dst, ssem, rsem, dev):
        copy = pltpu.make_async_remote_copy(
            src_ref=src, dst_ref=dst, send_sem=ssem, recv_sem=rsem, device_id=dev, device_id_type=MESH
        )
        copy.start()
        return copy

    def wait_all(copies):
        for copy in copies:
            copy.wait_recv()

    row = lax.broadcasted_iota(jnp.int32, (256, 256), 0)
    col = lax.broadcasted_iota(jnp.int32, (256, 256), 1)
    diff_n[...] = (row - (col & 15)).astype(F32)
    for copy in early:
        copy.wait()
    coup_in = load(coup_h, coup)
    near_in = load(near_h, near)
    for h in range(16):
        xl[h * 32 : h * 32 + 16, :] = inp[:, h * 256 : (h + 1) * 256]
        xl[h * 32 + 16 : h * 32 + 32, :] = adj[:, h * 256 : (h + 1) * 256]
    lists[0] = jnp.broadcast_to(slist[...], (8, 128))

    def leaves_in(step, carry):
        for i in range(4):
            leaf = step * 4 + i
            off = pl.multiple_of(leaf * 256, 256)
            places = pmap[:, pl.ds(off, 256)]
            low, high = places & 255, places >> 8
            hot = jnp.where(lax.broadcasted_iota(jnp.int32, (256, 256), 0) == low, 1.0, 0.0).astype(BF16)
            oh[:, pl.ds(off, 256)] = hot
            every = nn(xl[...], hot)
            vals = jnp.zeros((32, 256), F32)
            for h in range(16):
                vals = vals + jnp.where(high == h, every[h * 32 : (h + 1) * 32, :], 0.0)
            gath[leaf] = vals.astype(BF16)
        return carry

    lax.fori_loop(0, 4, leaves_in, 0)
    bases_in.wait()
    skel = batch_nt(gath[...], bases[...]).astype(BF16)
    ag0[...] = skel[:, :16]
    ws[...] = skel[:, 16:]

    pl.semaphore_wait(barrier, 17)
    cw_in, cc_in = [], []

    def ag_cw(k):
        dst = 4 if k == 3 else -(k + 1)
        cw_in.append(send(ag[FPOS[-k]], ag[FPOS[dst]], ag_s.at[k], ag_r.at[k], z_dev[1]))

    def ag_cc(k):
        cc_in.append(send(ag[FPOS[k]], ag[FPOS[k + 1]], ag_s.at[4 + k], ag_r.at[4 + k], z_dev[-1]))

    ag_cw(0)
    ag_cc(0)
    list_in = []
    for i, d in enumerate((1, -1, 2, -2, 3, -3, 4)):
        origin = 4 if d == 4 else -d
        list_in.append(send(lists.at[0], lists.at[FPOS[origin]], list_s.at[i], list_r.at[i], z_dev[d]))

    trans_in.wait()
    xd = jnp.zeros((16, 128), F32)
    wd = jnp.zeros((16, 128), F32)
    for leaf in range(16):
        xd = xd + nt(skel[leaf, :16], trans[leaf])
        wd = wd + nn(skel[leaf, 16:], trans[leaf])
    for copy in maps_in:
        copy.wait()
    xd2, wd2 = stacked(xd), stacked(wd)
    for v in range(6):
        cx = folded(nt(xd2, up[v]))
        cw = folded(nn(wd2, down[v]))
        lxs[0, v] = cx[:8]
        lxs[1, v] = cx[8:]
        lxs[2, v] = cw[:8]
        lxs[3, v] = cw[8:]
    lx_in = [
        send(lxs.at[b_at[d]], lxr.at[d - 1], lx_s.at[d - 1], lx_r.at[d - 1], x_dev[d]) for d in range(1, 4)
    ]

    f_in, b_in = [], []

    def plane_send(buf_s, buf_r, lo, hi, sems_s, sems_r, k):
        copies = []
        for e in range(1, 8):
            copies.append(
                send(
                    buf_s.at[w_at[e], pl.ds(lo, hi - lo)],
                    buf_r.at[w, pl.ds(lo, hi - lo)],
                    sems_s.at[k, e - 1],
                    sems_r.at[k, e - 1],
                    w_dev[e],
                )
            )
        buf_r[w, lo:hi] = buf_s[w, lo:hi]
        return copies

    tsm_in.wait()
    coup_in.wait()

    def b_batch(k):
        lo, hi = BBATCH[k]
        for pos in range(lo, hi):
            first = z_at[BWD[pos]] * 16
            for i in range(16):
                ret = nn(ws[tsm[0, first + i]], coup[first + i]).astype(BF16)
                bsend[i // 2, pos, (i % 2) * 16 : (i % 2) * 16 + 16] = ret
        b_in.append(plane_send(bsend, brecv, lo, hi, b_s, b_r, k))

    b_batch(0)
    b_batch(1)

    lane = lax.broadcasted_iota(jnp.int32, (8, 128), 1)
    spread = (
        (lax.broadcasted_iota(jnp.int32, (128, 256), 0) & 15) == (lax.broadcasted_iota(jnp.int32, (128, 256), 1) >> 4)
    ).astype(F32).astype(BF16)
    turn = (lax.broadcasted_iota(jnp.int32, (8, 128), 0) + z) & 7
    t_rows = jnp.broadcast_to(tlist[...], (8, 128))
    t_line = nn(jnp.where((lane >> 4) == turn, t_rows * 16, 0).astype(F32).astype(BF16), spread)

    def sum_matrix(line):
        return jnp.where(diff_n[...] == line, 1.0, 0.0).astype(BF16)

    def select(pos):
        for i in range(16):
            leaf = lsm[pos, 0, z * 16 + i]
            fsend[i // 2, pos, (i % 2) * 16 : (i % 2) * 16 + 16] = ag[pos][leaf]

    def f_batch(k):
        lo, hi = FBATCH[k]
        for pos in range(lo, hi):
            select(pos)
        f_in.append(plane_send(fsend, frecv, lo, hi, f_s, f_r, k))

    rs_cw, rs_cc = [], []

    def rs_cw_send(k, value):
        cws[k] = value.astype(BF16)
        rs_cw.append(send(cws.at[k], cwr.at[k], cw_s.at[k], cw_r.at[k], z_dev[1]))

    def rs_cc_send(k, value):
        ccs[k] = value.astype(BF16)
        rs_cc.append(send(ccs.at[k], ccr.at[k], cc_s.at[k], cc_r.at[k], z_dev[-1]))

    def list_chunk(pos, total):
        delta = FWD[pos]
        inc = frecv[:, pos].reshape(16, 16, 128)
        mats = coup[pl.ds(pl.multiple_of(z_at[delta] * 16, 16), 16)]
        terms = batch_nt(inc, mats).reshape(256, 128)
        high, low = split(terms)
        r = delta % 8
        both = nn(sum_matrix(t_line[r : r + 1]), jnp.concatenate([high, low], axis=1))
        return total + both[:, :128] + both[:, 128:]

    cw_in[0].wait_recv()
    ag_cw(1)
    cc_in[0].wait_recv()
    ag_cc(1)
    wait_all(list_in)
    lists_in = load(lists, lsm)
    b_batch(2)

    l_line = nn(
        jnp.where((lane >> 4) == z, lists[:, 0, :] * 16, 0).astype(F32).astype(BF16), spread
    )

    def part(delta):
        pos = FPOS[delta]
        return nn(sum_matrix(l_line[pos : pos + 1]), brecv[:, BPOS[delta]].reshape(256, 128))

    wait_all(lx_in)
    mine = lxs[b] + lxr[0] + lxr[1] + lxr[2]
    for v in range(3):
        lws[v, 0] = mine[v]
        lws[v, 1:4] = mine[3:6]
    lw_in = [
        send(lws.at[level_of(e)], lwr.at[e - 1], lw_s.at[e - 1], lw_r.at[e - 1], w_dev[e]) for e in range(1, 8)
    ]

    lists_in.wait()
    f_batch(0)
    b_batch(3)

    wait_all(b_in[0])
    rs_cc_send(0, part(4))
    wait_all(b_in[1])
    rs_cw_send(0, part(3))
    here_m3 = part(-3)

    near_in.wait()
    nx[...] = batch_nt(gath[:, :16], near[...])

    cw_in[1].wait_recv()
    ag_cw(2)
    cc_in[1].wait_recv()
    ag_cc(2)

    wait_all(lw_in)
    upper = mine[3:6]
    for e in range(1, 8):
        upper = upper + lwr[e - 1, 1:4]
    for v in range(3):
        lzs[v] = upper[v]
    lz_in = [send(lzs.at[level_of(e)], lzr.at[e - 1], lz_s.at[e - 1], lz_r.at[e - 1], zx_dev[e]) for e in range(1, 8)]

    wait_all(b_in[2])
    here_p, here_m = part(2), part(-2)
    rs_cc[0].wait_recv()
    rs_cc_send(1, here_m3 + ccr[0].astype(F32))
    rs_cw[0].wait_recv()
    rs_cw_send(1, here_p + cwr[0].astype(F32))

    nw[...] = batch_nn(gath[:, 16:], near[...])
    unit = jnp.where(row == col, 1.0, 0.0).astype(BF16)
    for leaf in range(16):
        oh_t[leaf * 256 : (leaf + 1) * 256, :] = lax.dot_general(
            oh[:, leaf * 256 : (leaf + 1) * 256], unit, (((0,), (0,)), ((), ())), preferred_element_type=F32
        ).astype(BF16)

    cw_in[2].wait_recv()
    ag_cw(3)
    cc_in[2].wait_recv()
    f_batch(1)

    wait_all(lz_in)
    quarter = [
        lwr[0, 0],
        lwr[1, 0] + lwr[2, 0],
        lwr[3, 0] + lwr[4, 0] + lwr[5, 0] + lwr[6, 0],
        lzr[0],
        lzr[1] + lzr[2],
        lzr[3] + lzr[4] + lzr[5] + lzr[6],
    ]
    for v in range(6):
        lar[b, v] = quarter[v]
    la_in = [send(lar.at[b], lar.at[b], la_s.at[d - 1], la_r.at[d - 1], x_dev[d]) for d in range(1, 4)]

    wait_all(b_in[3])
    here_p1, here_m1, own = part(1), part(-1), part(0)
    rs_cc[1].wait_recv()
    rs_cc_send(2, here_m + ccr[1].astype(F32))
    rs_cw[1].wait_recv()
    rs_cw_send(2, here_p1 + cwr[1].astype(F32))

    wait_all(f_in[0])
    lx = jnp.zeros((256, 128), F32)
    for pos in range(0, 3):
        lx = list_chunk(pos, lx)

    cw_in[3].wait_recv()
    f_batch(2)

    wait_all(la_in)
    yd = jnp.zeros((32, 128), F32)
    zd = jnp.zeros((32, 128), F32)
    for v in range(6):
        sx = jnp.concatenate([lar[0, v], lar[1, v]], axis=0)
        sw = jnp.concatenate([lar[2, v], lar[3, v]], axis=0)
        yd = yd + nt(stacked(sx), down[v])
        zd = zd + nn(stacked(sw), up[v])
    yd2, zd2 = stacked(folded(yd)), stacked(folded(zd))
    y_leaf = jnp.stack([folded(nn(yd2, trans[leaf])) for leaf in range(16)], axis=0)
    z_leaf = jnp.stack([folded(nt(zd2, trans[leaf])) for leaf in range(16)], axis=0)

    wait_all(f_in[1])
    for pos in range(3, 5):
        lx = list_chunk(pos, lx)

    rs_cc[2].wait_recv()
    rs_cc_send(3, here_m1 + ccr[2].astype(F32))

    for pos in range(5, 7):
        lx = list_chunk(pos, lx)

    def place(exp, near_term, out):
        vals = (batch_nn(exp.astype(BF16), bases[...]) + near_term[...]).astype(BF16).astype(F32)
        for leaf in range(16):
            high = pmap[:, leaf * 256 : (leaf + 1) * 256] >> 8
            marked[:, leaf * 256 : (leaf + 1) * 256] = jnp.concatenate(
                [jnp.where(high == h, vals[leaf], 0.0) for h in range(16)], axis=0
            ).astype(BF16)
        res = nn(marked[...], oh_t[...]).astype(BF16)
        for h in range(16):
            out[:, h * 256 : (h + 1) * 256] = res[h * 16 : h * 16 + 16]

    wait_all(f_in[2])
    lx = list_chunk(7, lx)
    place(y_leaf + lx.reshape(16, 16, 128), nx, out_x)

    rs_cw[2].wait_recv()
    rs_cc[3].wait_recv()
    lw = own + cwr[2].astype(F32) + ccr[3].astype(F32)
    place(z_leaf + lw.reshape(16, 16, 128), nw, out_a)

    for copies in [list_in, cw_in, cc_in, lx_in, lw_in, lz_in, la_in, rs_cw, rs_cc] + f_in + b_in:
        for copy in copies:
            copy.wait_send()


def hand_over(x_ref, a_ref, out_x, out_a):
    out_x[...] = x_ref[...]
    out_a[...] = a_ref[...]


def shards(inputs, adjoint_in, panel_map, bases, near, trans, up, down, send_list, target_leaf, coup):
    vmem = pl.BlockSpec(memory_space=pltpu.VMEM)
    hbm = pl.BlockSpec(memory_space=pltpu.HBM)
    dma = pltpu.SemaphoreType.DMA
    both = pl.pallas_call(
        kernel,
        out_shape=(jax.ShapeDtypeStruct((16, 4096), BF16), jax.ShapeDtypeStruct((16, 4096), BF16)),
        in_specs=[hbm] * 11,
        out_specs=(vmem, vmem),
        scratch_shapes=[
            pltpu.VMEM((16, 4096), BF16),
            pltpu.VMEM((16, 4096), BF16),
            pltpu.VMEM((1, 4096), jnp.int32),
            pltpu.VMEM((1, 128), jnp.int32),
            pltpu.VMEM((1, 128), jnp.int32),
            pltpu.VMEM((16, 128, 256), BF16),
            pltpu.VMEM((16, 256, 256), BF16),
            pltpu.VMEM((16, 128, 128), BF16),
            pltpu.VMEM((6, 128, 128), BF16),
            pltpu.VMEM((6, 128, 128), BF16),
            pltpu.VMEM((128, 128, 128), BF16),
            pltpu.SMEM((1, 128), jnp.int32),
            pltpu.SMEM((8, 8, 128), jnp.int32),
            pltpu.VMEM((512, 256), BF16),
            pltpu.VMEM((256, 4096), BF16),
            pltpu.VMEM((4096, 256), BF16),
            pltpu.VMEM((16, 32, 256), BF16),
            pltpu.VMEM((16, 16, 256), F32),
            pltpu.VMEM((16, 16, 256), F32),
            pltpu.VMEM((256, 256), F32),
            pltpu.VMEM((256, 4096), BF16),
        ]
        + [pltpu.VMEM((16, 16, 128), BF16)] * 8
        + [
            pltpu.VMEM((16, 16, 128), BF16),
            pltpu.VMEM((8, 8, 128), jnp.int32),
            pltpu.VMEM((8, 8, 32, 128), BF16),
            pltpu.VMEM((8, 8, 32, 128), BF16),
            pltpu.VMEM((8, 8, 32, 128), BF16),
            pltpu.VMEM((8, 8, 32, 128), BF16),
            pltpu.VMEM((3, 256, 128), BF16),
            pltpu.VMEM((3, 256, 128), BF16),
            pltpu.VMEM((4, 256, 128), BF16),
            pltpu.VMEM((4, 256, 128), BF16),
            pltpu.VMEM((4, 6, 8, 128), F32),
            pltpu.VMEM((3, 6, 8, 128), F32),
            pltpu.VMEM((3, 4, 8, 128), F32),
            pltpu.VMEM((7, 4, 8, 128), F32),
            pltpu.VMEM((3, 8, 128), F32),
            pltpu.VMEM((7, 8, 128), F32),
            pltpu.VMEM((4, 6, 8, 128), F32),
            dma((13,)),
            dma((7,)), dma((7,)),
            dma((7,)), dma((7,)),
            dma((4, 7)), dma((4, 7)),
            dma((4, 7)), dma((4, 7)),
            dma((3,)), dma((3,)),
            dma((4,)), dma((4,)),
            dma((3,)), dma((3,)),
            dma((7,)), dma((7,)),
            dma((7,)), dma((7,)),
            dma((3,)), dma((3,)),
        ],
        compiler_params=pltpu.CompilerParams(
            collective_id=0, has_side_effects=True, vmem_limit_bytes=60 * 1024 * 1024
        ),
    )(inputs, adjoint_in, panel_map, send_list, target_leaf, bases, near, trans, up, down, coup)
    shape = jax.ShapeDtypeStruct((16, 4096), BF16)
    return pl.pallas_call(hand_over, out_shape=(shape, shape), in_specs=[vmem] * 2, out_specs=(vmem, vmem))(*both)


def solution(mesh):
    each = ("sub", "blk")
    return jax.shard_map(
        shards,
        mesh=mesh,
        in_specs=(
            P(None, each),
            P(None, each),
            P(each, None),
            P(each, None, None),
            P(each, None, None),
            P(each, None, None),
            P(each, None, None),
            P(each, None, None),
            P(each, None),
            P(each, None),
            P(each, None, None),
        ),
        out_specs=(P(None, each), P(None, each)),
        check_vma=False,
    )
```
